256 devices in a mesh: fsdp: 16 (over y_hi, x, core), seq: 16 (over z, y_lo).
Axes of the slice: x: 4, y: 4 (y_hi: 2, y_lo: 2; y = y_hi * 2 + y_lo), z: 8, core: 2. Of those that a mesh axis runs over, the one named last changes fastest.
Arguments:
- queries: bfloat16 [16, 2048, 4096], P('fsdp', 'seq'), may hold values from -8 to 8
- key_states: bfloat16 [16, 2048, 4096], P('fsdp', 'seq'), may hold values from -8 to 8
- value_states: bfloat16 [16, 2048, 4096], P('fsdp', 'seq'), may hold values from -6 to 6
- query_tangent: bfloat16 [16, 2048, 4096], P('fsdp', 'seq'), may hold values from -6 to 6
- key_tangent: bfloat16 [16, 2048, 4096], P('fsdp', 'seq'), may hold values from -6 to 6
- value_tangent: bfloat16 [16, 2048, 4096], P('fsdp', 'seq'), may hold values from -6 to 6
- gate_table: float32 [1024, 4096], P('fsdp'), may hold values from 0.5 to 1.5
- rate_table: float32 [1024, 4096], P('fsdp'), may hold values from -4 to 4
- timesteps: int32 [16, 2], replicated, may hold values from 0 to 1023
- lengths: int32 [16, 2], P('fsdp'), may hold values from 512 to 1536, as said below
Outputs:
- attended: bfloat16 [16, 2048, 4096], P('fsdp', 'seq')
- attended_tangent: bfloat16 [16, 2048, 4096], P('fsdp', 'seq')
The draws below stay inside these ranges and needn't reach their ends.
Inputs may be any that keep to these rules, and one draw needn't show every extreme that they name: Each pack's two lengths sum to 2048.
All inputs are finite; a program needn't handle non-finite values.
Results may differ from the reference program's by a relative error of at most 0.0076.
Values may be sent and summed in bfloat16 or wider, within the bound.
No kernel may reach another device: no remote copies, remote signals or barrier semaphores. Data moves between devices by JAX's collectives and lax.ppermute only.
A program may use at most 128 MiB of HBM per device.

```python
import math
import jax
import jax.numpy as jnp
from jax import lax

HDIM = 128
HEADS = 32
SEQ_LEN = 2048
PACKS = 16
STEPS = 1024


def draw_queries(key, part):
    key = jax.random.fold_in(key, 3)
    base = jnp.clip(1.4 * jax.random.normal(key, (PACKS, SEQ_LEN, HEADS, HDIM), dtype=jnp.float32), -8.0, 8.0)
    return base.reshape(PACKS, SEQ_LEN, HEADS * HDIM).astype(jnp.bfloat16)


def draw_key_states(key, part):
    key = jax.random.fold_in(key, 5)
    base = jnp.clip(1.4 * jax.random.normal(key, (PACKS, SEQ_LEN, HEADS, HDIM), dtype=jnp.float32), -8.0, 8.0)
    return base.reshape(PACKS, SEQ_LEN, HEADS * HDIM).astype(jnp.bfloat16)


def draw_lengths(key, part):
    key = jax.random.fold_in(key, 11)
    first_key, order_key = jax.random.split(key)
    quarter = SEQ_LEN // 4
    first = jax.random.randint(first_key, (PACKS,), quarter, 3 * quarter + 1)
    order = jax.random.permutation(order_key, PACKS)
    first = first.at[order[0]].set(3 * quarter)
    first = first.at[order[1]].set(quarter)
    return jnp.stack([first, SEQ_LEN - first], axis=1).astype(jnp.int32)


def set_ends(values, key, low, top_value):
    index_at = [jax.random.randint(jax.random.fold_in(key, axis), (), 0, length) for axis, length in enumerate(values.shape)]
    main_axis = values.shape.index(max(values.shape))
    beside = index_at[:main_axis] + [(index_at[main_axis] + 1) % values.shape[main_axis]] + index_at[main_axis + 1:]
    return values.at[tuple(index_at)].set(low).at[tuple(beside)].set(top_value)


def block_scale(rng, shape, cuts, smallest, high):
    gain, own = 1.0, jax.random.fold_in(rng, 6)
    for dim, shards_of in cuts:
        steps = jnp.exp(jax.random.uniform(jax.random.fold_in(own, dim), (shards_of,), jnp.float32, smallest / len(cuts), high / len(cuts)))
        gain = gain * jnp.repeat(steps, shape[dim] // shards_of).reshape([-1 if axis == dim else 1 for axis in range(len(shape))])
    return gain


def centred(stream_key, shape, spread, most, shards=(), held_as=jnp.bfloat16):
    loudness = block_scale(stream_key, shape, shards, -0.22, 0.18) if shards else 1.0
    values = jax.random.normal(stream_key, shape, jnp.float32) * spread * loudness
    return jnp.minimum(jnp.maximum(values, -most), most).astype(held_as)


def setup_inputs(seed: int = 0) -> dict:
    key_of = jax.random.split(jax.random.key(seed), 11)
    return {
        "queries": draw_queries(jax.random.fold_in(key_of[10], 71), 0),
        "key_states": draw_key_states(jax.random.fold_in(key_of[10], 71), 0),
        "value_states": centred(key_of[2], (PACKS, SEQ_LEN, HEADS * HDIM), 1.0, 6.0, ((0, 16), (1, 16))),
        "query_tangent": centred(key_of[3], (PACKS, SEQ_LEN, HEADS * HDIM), 1.0, 6.0, ((0, 16), (1, 16))),
        "key_tangent": centred(key_of[4], (PACKS, SEQ_LEN, HEADS * HDIM), 1.0, 6.0, ((0, 16), (1, 16))),
        "value_tangent": centred(key_of[5], (PACKS, SEQ_LEN, HEADS * HDIM), 1.0, 6.0, ((0, 16), (1, 16))),
        "gate_table": jnp.clip(0.5 + 1.0 * jax.random.uniform(key_of[6], (STEPS, HEADS * HDIM), jnp.float32) ** block_scale(key_of[6], (STEPS, HEADS * HDIM), ((0, 16),), -0.2, 0.2), 0.5, 1.5),
        "rate_table": centred(key_of[7], (STEPS, HEADS * HDIM), 1.0, 4.0, ((0, 16),), jnp.float32),
        "timesteps": set_ends(jax.random.randint(key_of[8], (PACKS, 2), 0, STEPS), jax.random.fold_in(key_of[8], 1), 0, STEPS - 1).astype(jnp.int32),
        "lengths": draw_lengths(jax.random.fold_in(key_of[10], 71), 0),
    }


def primal_block(query_rows, row_sample, key_rows, value_rows, key_sample, score_scale):
    scores = jnp.einsum('qd,kd->qk', query_rows, key_rows, preferred_element_type=jnp.float32) * score_scale
    same_sample = row_sample[:, None] == key_sample[None, :]
    scores = jnp.where(same_sample, scores, -jnp.inf)
    row_max = lax.optimization_barrier(jnp.max(scores, axis=1, keepdims=True))
    exp_scores = jnp.exp(scores - row_max)
    weights = (exp_scores / lax.optimization_barrier(jnp.sum(exp_scores, axis=1, keepdims=True))).astype(jnp.bfloat16)
    output = jnp.dot(weights, value_rows, preferred_element_type=jnp.float32).astype(jnp.bfloat16)
    return (output, weights)

def tangent_block(weights, query_rows, tangent_rows, key_rows, key_moves, value_rows, value_moves, score_scale):
    score_tangent = jnp.einsum('qd,kd->qk', tangent_rows, key_rows, preferred_element_type=jnp.float32)
    score_tangent = (score_tangent + jnp.einsum('qd,kd->qk', query_rows, key_moves, preferred_element_type=jnp.float32)) * score_scale
    weights_wide = lax.optimization_barrier(weights).astype(jnp.float32)
    centre = lax.optimization_barrier(jnp.sum(weights_wide * score_tangent, axis=1, keepdims=True))
    weight_tangent = (weights_wide * (score_tangent - centre)).astype(jnp.bfloat16)
    result = jnp.dot(weight_tangent, value_rows, preferred_element_type=jnp.float32)
    result = result + jnp.dot(weights, value_moves, preferred_element_type=jnp.float32)
    return result.astype(jnp.bfloat16)

def reference(queries, key_states, value_states, query_tangent, key_tangent, value_tangent, gate_table, rate_table, timesteps, lengths):
    score_scale = 1.0 / math.sqrt(HDIM)

    def one_pack(pack_args):
        pack_q, pack_k, pack_v, pack_qt, pack_kt, pack_vt, step_pair, first_len = pack_args
        length = pack_q.shape[0]
        sample_id = (jnp.arange(length, dtype=jnp.int32) >= first_len).astype(jnp.int32)

        def to_heads(array):
            return array.reshape(length, HEADS, HDIM).transpose(1, 0, 2)

        def one_head(head_args):
            head_q, head_k, head_v, head_qt, head_kt, head_vt = head_args
            output, weights = primal_block(head_q, sample_id, head_k, head_v, sample_id, score_scale)
            moved = tangent_block(weights, head_q, head_qt, head_k, head_kt, head_v, head_vt, score_scale)
            return (output, moved)
        attention, attention_tangent = lax.map(one_head, (to_heads(pack_q), to_heads(pack_k), to_heads(pack_v), to_heads(pack_qt), to_heads(pack_kt), to_heads(pack_vt)))
        attention = attention.transpose(1, 0, 2).reshape(length, HEADS * HDIM).astype(jnp.float32)
        attention_tangent = attention_tangent.transpose(1, 0, 2).reshape(length, HEADS * HDIM).astype(jnp.float32)
        gate_pair = gate_table[step_pair]
        rate_pair = rate_table[step_pair]
        second = (sample_id == 1)[:, None]
        gate_rows = jnp.where(second, gate_pair[1][None, :], gate_pair[0][None, :])
        rate_rows = jnp.where(second, rate_pair[1][None, :], rate_pair[0][None, :])
        attended = (gate_rows * attention).astype(jnp.bfloat16)
        attended_tangent = (rate_rows * attention + gate_rows * attention_tangent).astype(jnp.bfloat16)
        return (attended, attended_tangent)
    return lax.map(one_pack, (queries, key_states, value_states, query_tangent, key_tangent, value_tangent, timesteps, lengths[:, 0]))
```

```python
import functools
import math

import jax
import jax.numpy as jnp
from jax import lax
from jax.experimental import pallas as pl
from jax.experimental.pallas import tpu as pltpu
from jax.sharding import PartitionSpec as P

HDIM = 128
BLOCK = 256
MASKED = -1e30


def pack_kernel(*refs):
    out_ref = refs[-1]
    for place, ref in enumerate(refs[:-1]):
        out_ref[0, place] = ref[0]


def pack_head(arrays, head, heads_here):
    _, tokens, width = arrays[0].shape
    groups = width // (heads_here * HDIM)
    count = len(arrays)
    return pl.pallas_call(
        pack_kernel,
        grid=(groups,),
        in_specs=[
            pl.BlockSpec((1, tokens, HDIM), lambda g: (0, 0, g * heads_here + head))
        ]
        * count,
        out_specs=pl.BlockSpec((1, count, tokens, HDIM), lambda g: (g, 0, 0, 0)),
        out_shape=jax.ShapeDtypeStruct((groups, count, tokens, HDIM), jnp.bfloat16),
        cost_estimate=pl.CostEstimate(
            flops=0, bytes_accessed=4 * count * groups * tokens * HDIM, transcendentals=0
        ),
    )(*arrays)


def unpack_kernel(*refs):
    heads = len(refs) - 2
    for head in range(heads):
        for place in range(2):
            refs[heads + place][0, :, head * HDIM : (head + 1) * HDIM] = refs[head][0, place]


def unpack(parts):
    groups, _, tokens, _ = parts[0].shape
    heads = len(parts)
    out = jax.ShapeDtypeStruct((1, tokens, groups * heads * HDIM), jnp.bfloat16)
    out_spec = pl.BlockSpec((1, tokens, heads * HDIM), lambda g: (0, 0, g))
    return pl.pallas_call(
        unpack_kernel,
        grid=(groups,),
        in_specs=[pl.BlockSpec((1, 2, tokens, HDIM), lambda g: (g, 0, 0, 0))] * heads,
        out_specs=[out_spec, out_spec],
        out_shape=[out, out],
        cost_estimate=pl.CostEstimate(
            flops=0, bytes_accessed=8 * heads * groups * tokens * HDIM, transcendentals=0
        ),
    )(*parts)


def attention_kernel(len_ref, in_ref, gate_ref, out_ref, kx, kk, vv, vo, scores, row_peak):
    groups, _, tokens, _ = in_ref.shape
    length = groups * tokens
    first_len = len_ref[0, 0]
    scale = 1.0 / math.sqrt(HDIM)
    exp2_scale = scale * math.log2(math.e)
    lane = lax.broadcasted_iota(jnp.int32, (tokens, HDIM), 1)
    ones = jnp.ones((tokens, HDIM), jnp.bfloat16)

    def fill(g, carry):
        rows = pl.ds(pl.multiple_of(g * tokens, tokens), tokens)
        key = in_ref[g, 1]
        value = in_ref[g, 2]
        place = g * tokens + lax.broadcasted_iota(jnp.int32, (tokens, HDIM), 0)
        other = jnp.where(place >= first_len, 0, 1)
        key_side = jnp.where(lane == other, MASKED, 0.0).astype(jnp.bfloat16)
        key_side = jnp.where(lane < 2, key_side, jnp.zeros_like(key_side))
        kx[rows, :HDIM] = key
        kx[rows, HDIM:] = key_side
        kk[rows, :HDIM] = key
        kk[rows, HDIM:] = in_ref[g, 4]
        vv[rows, :HDIM] = value
        vv[rows, HDIM:] = in_ref[g, 5]
        vo[rows, :HDIM] = value
        vo[rows, HDIM:] = ones
        return carry

    lax.fori_loop(0, groups, fill, 0)

    per = BLOCK // tokens
    nt = (((1,), (1,)), ((), ()))

    def one_block(block, carry):
        row0 = block * BLOCK
        query = in_ref[pl.ds(block * per, per), 0].reshape(BLOCK, HDIM)
        tangent = in_ref[pl.ds(block * per, per), 3].reshape(BLOCK, HDIM)
        place = row0 + lax.broadcasted_iota(jnp.int32, (BLOCK, HDIM), 0)
        second = place >= first_len
        own = jnp.where(second, 1, 0)
        lanes = lax.broadcasted_iota(jnp.int32, (BLOCK, HDIM), 1)
        query_side = jnp.where(lanes == own, 1.0, 0.0).astype(jnp.bfloat16)
        left = jnp.concatenate([query, query_side], axis=1)
        left_tangent = jnp.concatenate([tangent, query], axis=1)
        low = jnp.where(row0 >= first_len, first_len // BLOCK, 0)
        high = jnp.where(
            row0 + BLOCK <= first_len, (first_len + BLOCK - 1) // BLOCK, length // BLOCK
        )

        row_peak[...] = jnp.full((BLOCK, HDIM), -jnp.inf, jnp.float32)

        def first_pass(step, inner):
            rows = pl.ds(pl.multiple_of(step * BLOCK, BLOCK), BLOCK)
            found = lax.dot_general(left, kx[rows, :], nt, preferred_element_type=jnp.float32)
            scores[step] = found
            peak = row_peak[...]
            for cut in range(BLOCK // HDIM):
                peak = jnp.maximum(peak, found[:, cut * HDIM : (cut + 1) * HDIM])
            row_peak[...] = peak
            return inner

        lax.fori_loop(low, high, first_pass, 0)
        peak = jnp.max(row_peak[...], axis=1, keepdims=True)

        def second_pass(step, inner):
            total, sum_v, sum_t = inner
            rows = pl.ds(pl.multiple_of(step * BLOCK, BLOCK), BLOCK)
            weights = jnp.exp2((scores[step] - peak) * exp2_scale)
            moved = lax.dot_general(
                left_tangent, kk[rows, :], nt, preferred_element_type=jnp.float32
            )
            for cut in range(BLOCK // HDIM):
                total = total + weights[:, cut * HDIM : (cut + 1) * HDIM]
            sum_v = sum_v + jnp.dot(
                weights.astype(jnp.bfloat16), vv[rows, :], preferred_element_type=jnp.float32
            )
            sum_t = sum_t + jnp.dot(
                (weights * moved).astype(jnp.bfloat16),
                vo[rows, :],
                preferred_element_type=jnp.float32,
            )
            return total, sum_v, sum_t

        total, sum_v, sum_t = lax.fori_loop(
            low,
            high,
            second_pass,
            (
                jnp.zeros((BLOCK, HDIM), jnp.float32),
                jnp.zeros((BLOCK, 2 * HDIM), jnp.float32),
                jnp.zeros((BLOCK, 2 * HDIM), jnp.float32),
            ),
        )
        inverse = 1.0 / jnp.sum(total, axis=1, keepdims=True)
        plain = sum_v[:, :HDIM] * inverse
        centre = sum_t[:, HDIM:] * inverse
        moved = scale * (sum_t[:, :HDIM] * inverse - centre * plain) + sum_v[:, HDIM:] * inverse
        plain = plain.astype(jnp.bfloat16).astype(jnp.float32)
        moved = moved.astype(jnp.bfloat16).astype(jnp.float32)
        gate = jnp.where(second, gate_ref[1:2, :], gate_ref[0:1, :])
        rate = jnp.where(second, gate_ref[3:4, :], gate_ref[2:3, :])
        attended = (gate * plain).astype(jnp.bfloat16)
        attended_tangent = (rate * plain + gate * moved).astype(jnp.bfloat16)
        target = pl.ds(block * per, per)
        out_ref[target, 0] = attended.reshape(per, tokens, HDIM)
        out_ref[target, 1] = attended_tangent.reshape(per, tokens, HDIM)
        return carry

    lax.fori_loop(0, length // BLOCK, one_block, 0)


def attend(lengths, packed, gates):
    groups, _, tokens, _ = packed.shape
    length = groups * tokens
    wide = pltpu.VMEM((length, 2 * HDIM), jnp.bfloat16)
    return pl.pallas_call(
        attention_kernel,
        in_specs=[
            pl.BlockSpec(memory_space=pltpu.SMEM),
            pl.BlockSpec(memory_space=pltpu.VMEM),
            pl.BlockSpec(memory_space=pltpu.VMEM),
        ],
        out_specs=pl.BlockSpec(memory_space=pltpu.VMEM),
        out_shape=jax.ShapeDtypeStruct((groups, 2, tokens, HDIM), jnp.bfloat16),
        scratch_shapes=[
            wide,
            wide,
            wide,
            wide,
            pltpu.VMEM((length // BLOCK, BLOCK, BLOCK), jnp.float32),
            pltpu.VMEM((BLOCK, HDIM), jnp.float32),
        ],
        compiler_params=pltpu.CompilerParams(vmem_limit_bytes=32 * 1024 * 1024),
        cost_estimate=pl.CostEstimate(
            flops=8 * length * length * HDIM,
            bytes_accessed=16 * length * HDIM,
            transcendentals=length * length,
        ),
    )(lengths, packed, gates)


def exchange(array):
    return lax.all_to_all(array, "seq", split_axis=0, concat_axis=0, tiled=True)


def pick_gates(gate_table, rate_table, timesteps, groups):
    steps_here, width = gate_table.shape
    here = width // groups
    column = lax.axis_index("seq") * here
    tables = jnp.concatenate(
        [
            lax.dynamic_slice_in_dim(gate_table, column, here, 1),
            lax.dynamic_slice_in_dim(rate_table, column, here, 1),
        ],
        axis=1,
    )
    wanted = timesteps.reshape(-1) - lax.axis_index("fsdp") * steps_here
    one_hot = (wanted[:, None] == jnp.arange(steps_here, dtype=jnp.int32)[None, :]).astype(
        jnp.float32
    )
    picks = jnp.dot(one_hot, tables, precision=lax.Precision.HIGHEST)
    picks = picks.reshape(timesteps.shape[0], timesteps.shape[1], 2 * here)
    mine = lax.psum_scatter(picks, "fsdp", scatter_dimension=0, tiled=True)
    mine = mine.reshape(2, 2, here // HDIM, HDIM)
    return mine.transpose(2, 1, 0, 3).reshape(here // HDIM, 4, HDIM)


def on_device(
    queries,
    key_states,
    value_states,
    query_tangent,
    key_tangent,
    value_tangent,
    gate_table,
    rate_table,
    timesteps,
    lengths,
):
    groups = lax.axis_size("seq")
    heads_here = queries.shape[2] // (groups * HDIM)
    arrays = (queries, key_states, value_states, query_tangent, key_tangent, value_tangent)
    gates = pick_gates(gate_table, rate_table, timesteps, groups)
    parts = []
    for head in range(heads_here):
        received = exchange(pack_head(arrays, head, heads_here))
        parts.append(exchange(attend(lengths, received, gates[head])))
    return tuple(unpack(parts))


def solution(mesh):
    rows = P("fsdp", "seq", None)
    table = P("fsdp", None)
    in_specs = (rows,) * 6 + (table, table, P(), table)
    return jax.shard_map(
        on_device, mesh=mesh, in_specs=in_specs, out_specs=(rows, rows), check_vma=False
    )
```

```python
import functools
import math

import jax
import jax.numpy as jnp
from jax import lax
from jax.experimental import pallas as pl
from jax.experimental.pallas import tpu as pltpu
from jax.sharding import PartitionSpec as P

HDIM = 128
BLOCK = 256
GROUPS_A_STEP = 4
MASKED = -1e30


def pack_kernel(heads, *refs):
    arrays, parts = refs[:-heads], refs[-heads:]
    for place, ref in enumerate(arrays):
        for group in range(GROUPS_A_STEP):
            for head in range(heads):
                column = (group * heads + head) * HDIM
                parts[head][group, place] = ref[0, :, column : column + HDIM]


def pack(arrays, heads):
    _, tokens, width = arrays[0].shape
    groups = width // (heads * HDIM)
    count = len(arrays)
    part = jax.ShapeDtypeStruct((groups, count, tokens, HDIM), jnp.bfloat16)
    part_spec = pl.BlockSpec((GROUPS_A_STEP, count, tokens, HDIM), lambda g: (g, 0, 0, 0))
    row_spec = pl.BlockSpec((1, tokens, GROUPS_A_STEP * heads * HDIM), lambda g: (0, 0, g))
    return pl.pallas_call(
        functools.partial(pack_kernel, heads),
        grid=(groups // GROUPS_A_STEP,),
        in_specs=[row_spec] * count,
        out_specs=[part_spec] * heads,
        out_shape=[part] * heads,
        compiler_params=pltpu.CompilerParams(vmem_limit_bytes=32 * 1024 * 1024),
        cost_estimate=pl.CostEstimate(
            flops=0, bytes_accessed=4 * heads * count * groups * tokens * HDIM, transcendentals=0
        ),
    )(*arrays)


def unpack_kernel(*refs):
    heads = len(refs) - 2
    for head in range(heads):
        for group in range(GROUPS_A_STEP):
            column = (group * heads + head) * HDIM
            for place in range(2):
                refs[heads + place][0, :, column : column + HDIM] = refs[head][group, place]


def unpack(parts):
    groups, _, tokens, _ = parts[0].shape
    heads = len(parts)
    out = jax.ShapeDtypeStruct((1, tokens, groups * heads * HDIM), jnp.bfloat16)
    out_spec = pl.BlockSpec((1, tokens, GROUPS_A_STEP * heads * HDIM), lambda g: (0, 0, g))
    part_spec = pl.BlockSpec((GROUPS_A_STEP, 2, tokens, HDIM), lambda g: (g, 0, 0, 0))
    return pl.pallas_call(
        unpack_kernel,
        grid=(groups // GROUPS_A_STEP,),
        in_specs=[part_spec] * heads,
        out_specs=[out_spec, out_spec],
        out_shape=[out, out],
        compiler_params=pltpu.CompilerParams(vmem_limit_bytes=32 * 1024 * 1024),
        cost_estimate=pl.CostEstimate(
            flops=0, bytes_accessed=8 * heads * groups * tokens * HDIM, transcendentals=0
        ),
    )(*parts)


def attention_kernel(len_ref, in_ref, gate_ref, out_ref, kx, kk, vv, vo):
    groups, _, tokens, _ = in_ref.shape
    length = groups * tokens
    first_len = len_ref[0, 0]
    scale = 1.0 / math.sqrt(HDIM)
    exp2_scale = scale * math.log2(math.e)
    lane = lax.broadcasted_iota(jnp.int32, (tokens, HDIM), 1)
    ones = jnp.ones((tokens, HDIM), jnp.bfloat16)

    def fill(g, carry):
        rows = pl.ds(pl.multiple_of(g * tokens, tokens), tokens)
        key = in_ref[g, 1]
        value = in_ref[g, 2]
        place = g * tokens + lax.broadcasted_iota(jnp.int32, (tokens, HDIM), 0)
        other = jnp.where(place >= first_len, 0, 1)
        key_side = jnp.where(lane == other, MASKED, 0.0).astype(jnp.bfloat16)
        key_side = jnp.where(lane < 2, key_side, jnp.zeros_like(key_side))
        kx[rows, :HDIM] = key
        kx[rows, HDIM:] = key_side
        kk[rows, :HDIM] = key
        kk[rows, HDIM:] = in_ref[g, 4]
        vv[rows, :HDIM] = value
        vv[rows, HDIM:] = in_ref[g, 5]
        vo[rows, :HDIM] = value
        vo[rows, HDIM:] = ones
        return carry

    lax.fori_loop(0, groups, fill, 0)

    per = BLOCK // tokens
    nt = (((1,), (1,)), ((), ()))
    blocks = length // BLOCK

    def one_block(block, carry):
        row0 = block * BLOCK
        low = jnp.where(row0 >= first_len, first_len // BLOCK, 0)
        high = jnp.where(row0 + BLOCK <= first_len, (first_len + BLOCK - 1) // BLOCK, blocks)

        def with_width(width):
            query = in_ref[pl.ds(block * per, per), 0].reshape(BLOCK, HDIM)
            tangent = in_ref[pl.ds(block * per, per), 3].reshape(BLOCK, HDIM)
            place = row0 + lax.broadcasted_iota(jnp.int32, (BLOCK, HDIM), 0)
            second = place >= first_len
            own = jnp.where(second, 1, 0)
            lanes = lax.broadcasted_iota(jnp.int32, (BLOCK, HDIM), 1)
            query_side = jnp.where(lanes == own, 1.0, 0.0).astype(jnp.bfloat16)
            left = jnp.concatenate([query, query_side], axis=1)
            left_tangent = jnp.concatenate([tangent, query], axis=1)
            cuts = [
                pl.ds(pl.multiple_of((low + step) * BLOCK, BLOCK), BLOCK) for step in range(width)
            ]
            found = [
                lax.dot_general(left, kx[rows, :], nt, preferred_element_type=jnp.float32)
                for rows in cuts
            ]
            peak = functools.reduce(jnp.maximum, found)
            peak = jnp.max(peak, axis=1, keepdims=True)
            total = jnp.zeros((BLOCK, BLOCK), jnp.float32)
            plain_weights = []
            moved_weights = []
            for step, rows in enumerate(cuts):
                moved = lax.dot_general(
                    left_tangent, kk[rows, :], nt, preferred_element_type=jnp.float32
                )
                weights = jnp.exp2((found[step] - peak) * exp2_scale)
                total = total + weights
                plain_weights.append(weights.astype(jnp.bfloat16))
                moved_weights.append((weights * moved).astype(jnp.bfloat16))
            rows = pl.ds(pl.multiple_of(low * BLOCK, BLOCK), width * BLOCK)
            sum_v = jnp.dot(
                jnp.concatenate(plain_weights, axis=1),
                vv[rows, :],
                preferred_element_type=jnp.float32,
            )
            sum_t = jnp.dot(
                jnp.concatenate(moved_weights, axis=1),
                vo[rows, :],
                preferred_element_type=jnp.float32,
            )
            inverse = 1.0 / jnp.sum(total, axis=1, keepdims=True)
            plain = sum_v[:, :HDIM] * inverse
            centre = sum_t[:, HDIM:] * inverse
            moved = scale * (sum_t[:, :HDIM] * inverse - centre * plain)
            moved = moved + sum_v[:, HDIM:] * inverse
            plain = plain.astype(jnp.bfloat16).astype(jnp.float32)
            moved = moved.astype(jnp.bfloat16).astype(jnp.float32)
            gate = jnp.where(second, gate_ref[1:2, :], gate_ref[0:1, :])
            rate = jnp.where(second, gate_ref[3:4, :], gate_ref[2:3, :])
            attended = (gate * plain).astype(jnp.bfloat16)
            attended_tangent = (rate * plain + gate * moved).astype(jnp.bfloat16)
            target = pl.ds(block * per, per)
            out_ref[target, 0] = attended.reshape(per, tokens, HDIM)
            out_ref[target, 1] = attended_tangent.reshape(per, tokens, HDIM)

        for width in range(1, blocks + 1):
            pl.when(high - low == width)(functools.partial(with_width, width))
        return carry

    lax.fori_loop(0, blocks, one_block, 0)


def attend(lengths, packed, gates):
    groups, _, tokens, _ = packed.shape
    length = groups * tokens
    wide = pltpu.VMEM((length, 2 * HDIM), jnp.bfloat16)
    return pl.pallas_call(
        attention_kernel,
        in_specs=[
            pl.BlockSpec(memory_space=pltpu.SMEM),
            pl.BlockSpec(memory_space=pltpu.VMEM),
            pl.BlockSpec(memory_space=pltpu.VMEM),
        ],
        out_specs=pl.BlockSpec(memory_space=pltpu.VMEM),
        out_shape=jax.ShapeDtypeStruct((groups, 2, tokens, HDIM), jnp.bfloat16),
        scratch_shapes=[
            wide,
            wide,
            wide,
            wide,
        ],
        compiler_params=pltpu.CompilerParams(vmem_limit_bytes=32 * 1024 * 1024),
        cost_estimate=pl.CostEstimate(
            flops=8 * length * length * HDIM,
            bytes_accessed=16 * length * HDIM,
            transcendentals=length * length,
        ),
    )(lengths, packed, gates)


def exchange(array):
    return lax.all_to_all(array, "seq", split_axis=0, concat_axis=0, tiled=True)


def pick_gates(gate_table, rate_table, timesteps, groups):
    steps_here, width = gate_table.shape
    here = width // groups
    column = lax.axis_index("seq") * here
    tables = jnp.concatenate(
        [
            lax.dynamic_slice_in_dim(gate_table, column, here, 1),
            lax.dynamic_slice_in_dim(rate_table, column, here, 1),
        ],
        axis=1,
    )
    wanted = timesteps.reshape(-1) - lax.axis_index("fsdp") * steps_here
    one_hot = (wanted[:, None] == jnp.arange(steps_here, dtype=jnp.int32)[None, :]).astype(
        jnp.float32
    )
    picks = jnp.dot(one_hot, tables, precision=lax.Precision.HIGHEST)
    picks = picks.reshape(timesteps.shape[0], timesteps.shape[1], 2 * here)
    mine = lax.all_to_all(picks, "fsdp", split_axis=0, concat_axis=0, tiled=True).sum(axis=0)
    mine = mine.reshape(2, 2, here // HDIM, HDIM)
    return mine.transpose(2, 1, 0, 3).reshape(here // HDIM, 4, HDIM)


def on_device(
    queries,
    key_states,
    value_states,
    query_tangent,
    key_tangent,
    value_tangent,
    gate_table,
    rate_table,
    timesteps,
    lengths,
):
    groups = lax.axis_size("seq")
    heads_here = queries.shape[2] // (groups * HDIM)
    arrays = (queries, key_states, value_states, query_tangent, key_tangent, value_tangent)
    gates = pick_gates(gate_table, rate_table, timesteps, groups)
    parts = []
    for head, packed in enumerate(pack(arrays, heads_here)):
        parts.append(exchange(attend(lengths, exchange(packed), gates[head])))
    return tuple(unpack(parts))


def solution(mesh):
    rows = P("fsdp", "seq", None)
    table = P("fsdp", None)
    in_specs = (rows,) * 6 + (table, table, P(), table)
    return jax.shard_map(
        on_device, mesh=mesh, in_specs=in_specs, out_specs=(rows, rows), check_vma=False
    )
```

```python
import functools
import math

import jax
import jax.numpy as jnp
from jax import lax
from jax.experimental import pallas as pl
from jax.experimental.pallas import tpu as pltpu
from jax.sharding import PartitionSpec as P

HDIM = 128
BLOCK = 256
GROUPS_A_STEP = 4
ARRAYS = 6
MASKED = -1e30
WIDTHS = (2, 3, 4, 5, 6)
MIB = 1024 * 1024


def pack_kernel(heads, *refs):
    arrays, parts = refs[:-heads], refs[-heads:]
    for place, ref in enumerate(arrays):
        for group in range(GROUPS_A_STEP):
            for head in range(heads):
                column = (group * heads + head) * HDIM
                parts[head][group, place] = ref[0, :, column : column + HDIM]


def pack(arrays, heads):
    _, tokens, width = arrays[0].shape
    groups = width // (heads * HDIM)
    part = (ARRAYS, tokens, HDIM)
    row_spec = pl.BlockSpec((1, tokens, GROUPS_A_STEP * heads * HDIM), lambda g: (0, 0, g))
    part_spec = pl.BlockSpec((GROUPS_A_STEP,) + part, lambda g: (g, 0, 0, 0))
    return pl.pallas_call(
        functools.partial(pack_kernel, heads),
        grid=(groups // GROUPS_A_STEP,),
        in_specs=[row_spec] * ARRAYS,
        out_specs=[part_spec] * heads,
        out_shape=[jax.ShapeDtypeStruct((groups,) + part, jnp.bfloat16)] * heads,
        compiler_params=pltpu.CompilerParams(vmem_limit_bytes=56 * MIB),
        cost_estimate=pl.CostEstimate(
            flops=0, bytes_accessed=4 * ARRAYS * tokens * width, transcendentals=0
        ),
    )(*arrays)


def unpack_kernel(*refs):
    heads = len(refs) - 2
    for head in range(heads):
        for group in range(GROUPS_A_STEP):
            column = (group * heads + head) * HDIM
            for place in range(2):
                refs[heads + place][0, :, column : column + HDIM] = refs[head][group, place]


def unpack(parts):
    groups, _, tokens, _ = parts[0].shape
    heads = len(parts)
    out = jax.ShapeDtypeStruct((1, tokens, groups * heads * HDIM), jnp.bfloat16)
    out_spec = pl.BlockSpec((1, tokens, GROUPS_A_STEP * heads * HDIM), lambda g: (0, 0, g))
    part_spec = pl.BlockSpec((GROUPS_A_STEP, 2, tokens, HDIM), lambda g: (g, 0, 0, 0))
    return pl.pallas_call(
        unpack_kernel,
        grid=(groups // GROUPS_A_STEP,),
        in_specs=[part_spec] * heads,
        out_specs=[out_spec, out_spec],
        out_shape=[out, out],
        compiler_params=pltpu.CompilerParams(vmem_limit_bytes=32 * MIB),
        cost_estimate=pl.CostEstimate(
            flops=0, bytes_accessed=8 * heads * groups * tokens * HDIM, transcendentals=0
        ),
    )(*parts)


def attention_kernel(len_ref, in_ref, gate_ref, query_side, key_side, out_ref):
    groups, _, tokens, _ = in_ref.shape
    length = groups * tokens
    first_len = len_ref[0, 0]
    scale = 1.0 / math.sqrt(HDIM)
    exp2_scale = scale * math.log2(math.e)
    nt = (((1,), (1,)), ((), ()))
    per = BLOCK // tokens
    blocks = length // BLOCK
    row = lax.broadcasted_iota(jnp.int32, (BLOCK, HDIM), 0)

    def rows_of(block, count, place):
        found = in_ref[pl.ds(block * per, count * per), place]
        return found.reshape(count * BLOCK, HDIM)

    def beside(*pieces):
        return jnp.concatenate(pieces, axis=1)

    def one_block(block, carry):
        row0 = pl.multiple_of(block * BLOCK, BLOCK)
        second = row0 + row >= first_len
        low = jnp.where(row0 >= first_len, first_len // BLOCK, 0)
        high = jnp.where(row0 + BLOCK <= first_len, (first_len + BLOCK - 1) // BLOCK, blocks)

        def score(low, width):
            left = beside(rows_of(block, 1, 0), query_side[pl.ds(row0, BLOCK), :])
            found = []
            for step in range(width):
                start = pl.multiple_of((low + step) * BLOCK, BLOCK)
                right = beside(rows_of(low + step, 1, 1), key_side[pl.ds(start, BLOCK), :])
                found.append(
                    lax.dot_general(left, right, nt, preferred_element_type=jnp.float32)
                )
            halves = [f[:, i : i + HDIM] for f in found for i in range(0, BLOCK, HDIM)]
            peak = jnp.max(functools.reduce(jnp.maximum, halves), axis=1, keepdims=True)
            return found, peak

        def weigh(low, found, peak):
            left = beside(rows_of(block, 1, 3), rows_of(block, 1, 0))
            total = jnp.zeros((BLOCK, HDIM), jnp.float32)
            plain_weights = []
            moved_weights = []
            for step, scores in enumerate(found):
                right = beside(rows_of(low + step, 1, 1), rows_of(low + step, 1, 4))
                moved = lax.dot_general(left, right, nt, preferred_element_type=jnp.float32)
                weights = jnp.exp2((scores - peak) * exp2_scale)
                for i in range(0, BLOCK, HDIM):
                    total = total + weights[:, i : i + HDIM]
                plain_weights.append(weights.astype(jnp.bfloat16))
                moved_weights.append((weights * moved).astype(jnp.bfloat16))
            return total, beside(*plain_weights), beside(*moved_weights)

        def combine(low, width, plain_weights, moved_weights):
            value = rows_of(low, width, 2)
            sum_v = jnp.dot(
                plain_weights,
                beside(value, rows_of(low, width, 5)),
                preferred_element_type=jnp.float32,
            )
            sum_t = jnp.dot(
                moved_weights,
                beside(value, jnp.ones((width * BLOCK, HDIM), jnp.bfloat16)),
                preferred_element_type=jnp.float32,
            )
            return sum_v, sum_t

        def finish(total, sum_v, sum_t):
            inverse = 1.0 / jnp.sum(total, axis=1, keepdims=True)
            plain = sum_v[:, :HDIM] * inverse
            centre = sum_t[:, HDIM:] * inverse
            moved = scale * (sum_t[:, :HDIM] * inverse - centre * plain)
            moved = moved + sum_v[:, HDIM:] * inverse
            plain = plain.astype(jnp.bfloat16).astype(jnp.float32)
            moved = moved.astype(jnp.bfloat16).astype(jnp.float32)
            gate = jnp.where(second, gate_ref[1:2, :], gate_ref[0:1, :])
            rate = jnp.where(second, gate_ref[3:4, :], gate_ref[2:3, :])
            attended = (gate * plain).astype(jnp.bfloat16)
            attended_tangent = (rate * plain + gate * moved).astype(jnp.bfloat16)
            target = pl.ds(block * per, per)
            out_ref[target, 0] = attended.reshape(per, tokens, HDIM)
            out_ref[target, 1] = attended_tangent.reshape(per, tokens, HDIM)

        def with_width(width):
            first = jnp.minimum(low, blocks - width)
            found, peak = score(first, width)
            total, plain_weights, moved_weights = weigh(first, found, peak)
            finish(total, *combine(first, width, plain_weights, moved_weights))

        widths = [width for width in WIDTHS if width < blocks] + [blocks]
        for below, width in zip([0] + widths, widths):
            fits = (high - low > below) & (high - low <= width)
            pl.when(fits)(functools.partial(with_width, width))
        return carry

    lax.fori_loop(0, blocks, one_block, 0)


def sides(first_len, length):
    own = (jnp.arange(length, dtype=jnp.int32) >= first_len).astype(jnp.int32)[:, None]
    lane = jnp.arange(HDIM, dtype=jnp.int32)[None, :]
    query_side = jnp.where(lane == own, 1.0, 0.0).astype(jnp.bfloat16)
    key_side = jnp.where(lane == 1 - own, MASKED, 0.0).astype(jnp.bfloat16)
    return query_side, key_side


def attend(lengths, received, gates, query_side, key_side):
    groups, _, tokens, _ = received.shape
    length = groups * tokens
    in_vmem = pl.BlockSpec(memory_space=pltpu.VMEM)
    return pl.pallas_call(
        attention_kernel,
        in_specs=[pl.BlockSpec(memory_space=pltpu.SMEM)] + [in_vmem] * 4,
        out_specs=in_vmem,
        out_shape=jax.ShapeDtypeStruct((groups, 2, tokens, HDIM), jnp.bfloat16),
        compiler_params=pltpu.CompilerParams(vmem_limit_bytes=32 * MIB),
        cost_estimate=pl.CostEstimate(
            flops=8 * length * length * HDIM,
            bytes_accessed=16 * length * HDIM,
            transcendentals=length * length,
        ),
    )(lengths, received, gates, query_side, key_side)


def exchange(array):
    return lax.all_to_all(array, "seq", split_axis=0, concat_axis=0, tiled=True)


def pick_gates(gate_table, rate_table, timesteps, groups):
    steps_here, width = gate_table.shape
    here = width // groups
    column = lax.axis_index("seq") * here
    tables = jnp.concatenate(
        [
            lax.dynamic_slice_in_dim(gate_table, column, here, 1),
            lax.dynamic_slice_in_dim(rate_table, column, here, 1),
        ],
        axis=1,
    )
    me = lax.axis_index("fsdp")
    wanted = timesteps.reshape(-1) - me * steps_here
    one_hot = (wanted[:, None] == jnp.arange(steps_here, dtype=jnp.int32)[None, :]).astype(
        jnp.float32
    )
    picks = jnp.dot(one_hot, tables, precision=lax.Precision.HIGHEST)
    size = lax.axis_size("fsdp")
    picks = picks.reshape(size, -1)
    bit = size // 2
    while bit:
        mine = (me // bit) % 2
        halves = picks.reshape(2, bit, -1)
        kept = lax.dynamic_index_in_dim(halves, mine, 0, keepdims=False)
        sent = lax.dynamic_index_in_dim(halves, 1 - mine, 0, keepdims=False)
        picks = kept + lax.ppermute(sent, "fsdp", [(i, i ^ bit) for i in range(size)])
        bit //= 2
    mine = picks.reshape(2, 2, here // HDIM, HDIM)
    return mine.transpose(2, 1, 0, 3).reshape(here // HDIM, 4, HDIM)


def on_device(
    queries,
    key_states,
    value_states,
    query_tangent,
    key_tangent,
    value_tangent,
    gate_table,
    rate_table,
    timesteps,
    lengths,
):
    groups = lax.axis_size("seq")
    heads = queries.shape[2] // (groups * HDIM)
    arrays = (queries, key_states, value_states, query_tangent, key_tangent, value_tangent)
    packed = pack(arrays, heads)
    gates = pick_gates(gate_table, rate_table, timesteps, groups)
    query_side, key_side = sides(lengths[0, 0], groups * queries.shape[1])
    parts = []
    for head in range(heads):
        received = exchange(packed[head])
        parts.append(attend(lengths, received, gates[head], query_side, key_side))
    return tuple(unpack([exchange(part) for part in parts]))


def solution(mesh):
    rows = P("fsdp", "seq", None)
    table = P("fsdp", None)
    in_specs = (rows,) * 6 + (table, table, P(), table)
    return jax.shard_map(
        on_device, mesh=mesh, in_specs=in_specs, out_specs=(rows, rows), check_vma=False
    )
```

```python
import functools
import math

import jax
import jax.numpy as jnp
from jax import lax
from jax.experimental import pallas as pl
from jax.experimental.pallas import tpu as pltpu
from jax.sharding import PartitionSpec as P

HDIM = 128
BLOCK = 256
GROUPS_A_STEP = 4
ARRAYS = 6
MASKED = -1e30
WIDTHS = (2, 3, 4, 5, 6)
MIB = 1024 * 1024


def pack_kernel(*refs):
    part = refs[-1]
    for index, ref in enumerate(refs[: ARRAYS * GROUPS_A_STEP]):
        part[index % GROUPS_A_STEP, index // GROUPS_A_STEP] = ref[0]


def pack_head(arrays, heads, head, *after):
    _, tokens, width = arrays[0].shape
    groups = width // (heads * HDIM)
    part = (ARRAYS, tokens, HDIM)

    def column(turn):
        def place(i):
            return (0, 0, (i * GROUPS_A_STEP + turn) * heads + head)

        return pl.BlockSpec((1, tokens, HDIM), place)

    return pl.pallas_call(
        pack_kernel,
        grid=(groups // GROUPS_A_STEP,),
        in_specs=[column(turn) for turn in range(GROUPS_A_STEP)] * ARRAYS
        + [pl.BlockSpec(memory_space=pl.ANY)] * len(after),
        out_specs=pl.BlockSpec((GROUPS_A_STEP,) + part, lambda i: (i, 0, 0, 0)),
        out_shape=jax.ShapeDtypeStruct((groups,) + part, jnp.bfloat16),
        compiler_params=pltpu.CompilerParams(vmem_limit_bytes=60 * MIB),
        cost_estimate=pl.CostEstimate(
            flops=0, bytes_accessed=4 * ARRAYS * groups * tokens * HDIM, transcendentals=0
        ),
    )(*[array for array in arrays for _ in range(GROUPS_A_STEP)], *after)


def unpack_kernel(*refs):
    heads = len(refs) - 2
    for head in range(heads):
        for group in range(GROUPS_A_STEP):
            column = (group * heads + head) * HDIM
            for place in range(2):
                refs[heads + place][0, :, column : column + HDIM] = refs[head][group, place]


def unpack(parts):
    groups, _, tokens, _ = parts[0].shape
    heads = len(parts)
    out = jax.ShapeDtypeStruct((1, tokens, groups * heads * HDIM), jnp.bfloat16)
    out_spec = pl.BlockSpec((1, tokens, GROUPS_A_STEP * heads * HDIM), lambda g: (0, 0, g))
    part_spec = pl.BlockSpec((GROUPS_A_STEP, 2, tokens, HDIM), lambda g: (g, 0, 0, 0))
    return pl.pallas_call(
        unpack_kernel,
        grid=(groups // GROUPS_A_STEP,),
        in_specs=[part_spec] * heads,
        out_specs=[out_spec, out_spec],
        out_shape=[out, out],
        compiler_params=pltpu.CompilerParams(vmem_limit_bytes=32 * MIB),
        cost_estimate=pl.CostEstimate(
            flops=0, bytes_accessed=8 * heads * groups * tokens * HDIM, transcendentals=0
        ),
    )(*parts)


def attention_kernel(len_ref, in_ref, gate_ref, out_ref, query_side, key_side):
    groups, _, tokens, _ = in_ref.shape
    length = groups * tokens
    first_len = len_ref[0, 0]
    scale = 1.0 / math.sqrt(HDIM)
    exp2_scale = scale * math.log2(math.e)
    nt = (((1,), (1,)), ((), ()))
    per = BLOCK // tokens
    blocks = length // BLOCK
    row = lax.broadcasted_iota(jnp.int32, (BLOCK, HDIM), 0)
    lane = lax.broadcasted_iota(jnp.int32, (BLOCK, HDIM), 1)

    def fill(block, carry):
        start = pl.multiple_of(block * BLOCK, BLOCK)
        own = jnp.where(start + row >= first_len, 1, 0)
        rows = pl.ds(start, BLOCK)
        query_side[rows, :] = jnp.where(lane == own, 1.0, 0.0).astype(jnp.bfloat16)
        key_side[rows, :] = jnp.where(lane == 1 - own, MASKED, 0.0).astype(jnp.bfloat16)
        return carry

    lax.fori_loop(0, blocks, fill, 0)

    def rows_of(block, count, place):
        found = in_ref[pl.ds(block * per, count * per), place]
        return found.reshape(count * BLOCK, HDIM)

    def beside(*pieces):
        return jnp.concatenate(pieces, axis=1)

    def one_block(block, carry):
        row0 = pl.multiple_of(block * BLOCK, BLOCK)
        second = row0 + row >= first_len
        low = jnp.where(row0 >= first_len, first_len // BLOCK, 0)
        high = jnp.where(row0 + BLOCK <= first_len, (first_len + BLOCK - 1) // BLOCK, blocks)

        def score(low, width):
            left = beside(rows_of(block, 1, 0), query_side[pl.ds(row0, BLOCK), :])
            found = []
            for step in range(width):
                start = pl.multiple_of((low + step) * BLOCK, BLOCK)
                right = beside(rows_of(low + step, 1, 1), key_side[pl.ds(start, BLOCK), :])
                found.append(
                    lax.dot_general(left, right, nt, preferred_element_type=jnp.float32)
                )
            halves = [f[:, i : i + HDIM] for f in found for i in range(0, BLOCK, HDIM)]
            peak = jnp.max(functools.reduce(jnp.maximum, halves), axis=1, keepdims=True)
            return found, peak

        def weigh(low, found, peak):
            left = beside(rows_of(block, 1, 3), rows_of(block, 1, 0))
            total = jnp.zeros((BLOCK, HDIM), jnp.float32)
            plain_weights = []
            moved_weights = []
            for step, scores in enumerate(found):
                right = beside(rows_of(low + step, 1, 1), rows_of(low + step, 1, 4))
                moved = lax.dot_general(left, right, nt, preferred_element_type=jnp.float32)
                weights = jnp.exp2((scores - peak) * exp2_scale)
                for i in range(0, BLOCK, HDIM):
                    total = total + weights[:, i : i + HDIM]
                plain_weights.append(weights.astype(jnp.bfloat16))
                moved_weights.append((weights * moved).astype(jnp.bfloat16))
            return total, beside(*plain_weights), beside(*moved_weights)

        def combine(low, width, plain_weights, moved_weights):
            value = rows_of(low, width, 2)
            sum_v = jnp.dot(
                plain_weights,
                beside(value, rows_of(low, width, 5)),
                preferred_element_type=jnp.float32,
            )
            sum_t = jnp.dot(
                moved_weights,
                beside(value, jnp.ones((width * BLOCK, HDIM), jnp.bfloat16)),
                preferred_element_type=jnp.float32,
            )
            return sum_v, sum_t

        def finish(total, sum_v, sum_t):
            inverse = 1.0 / jnp.sum(total, axis=1, keepdims=True)
            plain = sum_v[:, :HDIM] * inverse
            centre = sum_t[:, HDIM:] * inverse
            moved = scale * (sum_t[:, :HDIM] * inverse - centre * plain)
            moved = moved + sum_v[:, HDIM:] * inverse
            plain = plain.astype(jnp.bfloat16).astype(jnp.float32)
            moved = moved.astype(jnp.bfloat16).astype(jnp.float32)
            gate = jnp.where(second, gate_ref[1:2, :], gate_ref[0:1, :])
            rate = jnp.where(second, gate_ref[3:4, :], gate_ref[2:3, :])
            attended = (gate * plain).astype(jnp.bfloat16)
            attended_tangent = (rate * plain + gate * moved).astype(jnp.bfloat16)
            target = pl.ds(block * per, per)
            out_ref[target, 0] = attended.reshape(per, tokens, HDIM)
            out_ref[target, 1] = attended_tangent.reshape(per, tokens, HDIM)

        def with_width(width):
            first = jnp.minimum(low, blocks - width)
            found, peak = score(first, width)
            total, plain_weights, moved_weights = weigh(first, found, peak)
            finish(total, *combine(first, width, plain_weights, moved_weights))

        widths = [width for width in WIDTHS if width < blocks] + [blocks]
        for below, width in zip([0] + widths, widths):
            fits = (high - low > below) & (high - low <= width)
            pl.when(fits)(functools.partial(with_width, width))
        return carry

    lax.fori_loop(0, blocks, one_block, 0)


def attend(lengths, received, gates):
    groups, _, tokens, _ = received.shape
    length = groups * tokens
    in_vmem = pl.BlockSpec(memory_space=pltpu.VMEM)
    return pl.pallas_call(
        attention_kernel,
        in_specs=[pl.BlockSpec(memory_space=pltpu.SMEM)] + [in_vmem] * 2,
        out_specs=in_vmem,
        out_shape=jax.ShapeDtypeStruct((groups, 2, tokens, HDIM), jnp.bfloat16),
        scratch_shapes=[pltpu.VMEM((length, HDIM), jnp.bfloat16)] * 2,
        compiler_params=pltpu.CompilerParams(vmem_limit_bytes=32 * MIB),
        cost_estimate=pl.CostEstimate(
            flops=8 * length * length * HDIM,
            bytes_accessed=16 * length * HDIM,
            transcendentals=length * length,
        ),
    )(lengths, received, gates)


def exchange(array):
    return lax.all_to_all(array, "seq", split_axis=0, concat_axis=0, tiled=True)


def pick_rows(gate_table, rate_table, timesteps, groups):
    steps_here, width = gate_table.shape
    here = width // groups
    column = lax.axis_index("seq") * here
    tables = jnp.concatenate(
        [
            lax.dynamic_slice_in_dim(gate_table, column, here, 1),
            lax.dynamic_slice_in_dim(rate_table, column, here, 1),
        ],
        axis=1,
    )
    wanted = timesteps.reshape(-1) - lax.axis_index("fsdp") * steps_here
    one_hot = (wanted[:, None] == jnp.arange(steps_here, dtype=jnp.int32)[None, :]).astype(
        jnp.float32
    )
    picks = jnp.dot(one_hot, tables, precision=lax.Precision.HIGHEST)
    return picks.reshape(timesteps.shape[0], -1)


def behind_kernel(array, after, out):
    out[...] = array[...]


def behind(array, after):
    in_vmem = pl.BlockSpec(memory_space=pltpu.VMEM)
    return pl.pallas_call(
        behind_kernel,
        in_specs=[in_vmem, pl.BlockSpec(memory_space=pl.ANY)],
        out_specs=in_vmem,
        out_shape=jax.ShapeDtypeStruct(array.shape, array.dtype),
    )(array, after)


def halve(picks, bit, members):
    mine = (lax.axis_index("fsdp") // bit) % 2
    split = picks.reshape(2, bit, -1)
    kept = lax.dynamic_index_in_dim(split, mine, 0, keepdims=False)
    sent = lax.dynamic_index_in_dim(split, 1 - mine, 0, keepdims=False)
    return kept + lax.ppermute(sent, "fsdp", [(i, i ^ bit) for i in members])


def sum_picks(picks, core):
    size = lax.axis_size("fsdp")
    bit = size // 2
    while bit > 1:
        picks = halve(picks, bit, range(core, size, 2))
        bit //= 2
    return picks


def on_device(
    queries,
    key_states,
    value_states,
    query_tangent,
    key_tangent,
    value_tangent,
    gate_table,
    rate_table,
    timesteps,
    lengths,
):
    groups = lax.axis_size("seq")
    heads = queries.shape[2] // (groups * HDIM)
    arrays = (queries, key_states, value_states, query_tangent, key_tangent, value_tangent)
    picks = pick_rows(gate_table, rate_table, timesteps, groups)
    odd_sum = sum_picks(picks, 1)
    packed = [pack_head(arrays, heads, 0, odd_sum)]
    for head in range(1, heads):
        packed.append(pack_head(arrays, heads, head, packed[-1]))
    even_sum = sum_picks(behind(picks, packed[-1]), 0)
    sums = jnp.where(lax.axis_index("fsdp") % 2 == 1, odd_sum, even_sum)
    mine = halve(sums, 1, range(lax.axis_size("fsdp")))
    mine = mine.reshape(2, 2, heads, HDIM)
    gates = mine.transpose(2, 1, 0, 3).reshape(heads, 4, HDIM)
    received = [exchange(part) for part in packed]
    parts = [attend(lengths, array, gate) for array, gate in zip(received, gates)]
    return tuple(unpack([exchange(part) for part in parts]))


def solution(mesh):
    rows = P("fsdp", "seq", None)
    table = P("fsdp", None)
    in_specs = (rows,) * 6 + (table, table, P(), table)
    return jax.shard_map(
        on_device, mesh=mesh, in_specs=in_specs, out_specs=(rows, rows), check_vma=False
    )
```

```python
import functools
import math

import jax
import jax.numpy as jnp
from jax import lax
from jax.experimental import pallas as pl
from jax.experimental.pallas import tpu as pltpu
from jax.sharding import PartitionSpec as P

HDIM = 128
BLOCK = 256
GROUPS_A_STEP = 4
ARRAYS = 6
MASKED = -1e30
WIDTHS = (2, 3, 4, 5, 6)
MIB = 1024 * 1024


def pack_kernel(heads, *refs):
    parts = refs[-heads:]
    for place, ref in enumerate(refs[:ARRAYS]):
        for group in range(GROUPS_A_STEP):
            for head in range(heads):
                column = (group * heads + head) * HDIM
                parts[head][group, place] = ref[0, :, column : column + HDIM]


def pack(arrays, heads, *after):
    _, tokens, width = arrays[0].shape
    groups = width // (heads * HDIM)
    part = (ARRAYS, tokens, HDIM)
    row_spec = pl.BlockSpec((1, tokens, GROUPS_A_STEP * heads * HDIM), lambda g: (0, 0, g))
    part_spec = pl.BlockSpec((GROUPS_A_STEP,) + part, lambda g: (g, 0, 0, 0))
    return pl.pallas_call(
        functools.partial(pack_kernel, heads),
        grid=(groups // GROUPS_A_STEP,),
        in_specs=[row_spec] * ARRAYS + [pl.BlockSpec(memory_space=pl.ANY)] * len(after),
        out_specs=[part_spec] * heads,
        out_shape=[jax.ShapeDtypeStruct((groups,) + part, jnp.bfloat16)] * heads,
        compiler_params=pltpu.CompilerParams(vmem_limit_bytes=56 * MIB),
        cost_estimate=pl.CostEstimate(
            flops=0, bytes_accessed=4 * ARRAYS * tokens * width, transcendentals=0
        ),
    )(*arrays, *after)


def unpack_kernel(*refs):
    heads = len(refs) - 2
    for head in range(heads):
        for group in range(GROUPS_A_STEP):
            column = (group * heads + head) * HDIM
            for place in range(2):
                refs[heads + place][0, :, column : column + HDIM] = refs[head][group, place]


def unpack(parts):
    groups, _, tokens, _ = parts[0].shape
    heads = len(parts)
    out = jax.ShapeDtypeStruct((1, tokens, groups * heads * HDIM), jnp.bfloat16)
    out_spec = pl.BlockSpec((1, tokens, GROUPS_A_STEP * heads * HDIM), lambda g: (0, 0, g))
    part_spec = pl.BlockSpec((GROUPS_A_STEP, 2, tokens, HDIM), lambda g: (g, 0, 0, 0))
    return pl.pallas_call(
        unpack_kernel,
        grid=(groups // GROUPS_A_STEP,),
        in_specs=[part_spec] * heads,
        out_specs=[out_spec, out_spec],
        out_shape=[out, out],
        compiler_params=pltpu.CompilerParams(vmem_limit_bytes=32 * MIB),
        cost_estimate=pl.CostEstimate(
            flops=0, bytes_accessed=8 * heads * groups * tokens * HDIM, transcendentals=0
        ),
    )(*parts)


def attention_kernel(len_ref, in_ref, gate_ref, out_ref, query_side, key_side):
    groups, _, tokens, _ = in_ref.shape
    length = groups * tokens
    first_len = len_ref[0, 0]
    scale = 1.0 / math.sqrt(HDIM)
    exp2_scale = scale * math.log2(math.e)
    nt = (((1,), (1,)), ((), ()))
    per = BLOCK // tokens
    blocks = length // BLOCK
    row = lax.broadcasted_iota(jnp.int32, (BLOCK, HDIM), 0)
    lane = lax.broadcasted_iota(jnp.int32, (BLOCK, HDIM), 1)

    def fill(block, carry):
        start = pl.multiple_of(block * BLOCK, BLOCK)
        own = jnp.where(start + row >= first_len, 1, 0)
        rows = pl.ds(start, BLOCK)
        query_side[rows, :] = jnp.where(lane == own, 1.0, 0.0).astype(jnp.bfloat16)
        key_side[rows, :] = jnp.where(lane == 1 - own, MASKED, 0.0).astype(jnp.bfloat16)
        return carry

    lax.fori_loop(0, blocks, fill, 0)

    def rows_of(block, count, place):
        found = in_ref[pl.ds(block * per, count * per), place]
        return found.reshape(count * BLOCK, HDIM)

    def beside(*pieces):
        return jnp.concatenate(pieces, axis=1)

    def one_block(block, carry):
        row0 = pl.multiple_of(block * BLOCK, BLOCK)
        second = row0 + row >= first_len
        low = jnp.where(row0 >= first_len, first_len // BLOCK, 0)
        high = jnp.where(row0 + BLOCK <= first_len, (first_len + BLOCK - 1) // BLOCK, blocks)

        def score(low, width):
            left = beside(rows_of(block, 1, 0), query_side[pl.ds(row0, BLOCK), :])
            found = []
            for step in range(width):
                start = pl.multiple_of((low + step) * BLOCK, BLOCK)
                right = beside(rows_of(low + step, 1, 1), key_side[pl.ds(start, BLOCK), :])
                found.append(
                    lax.dot_general(left, right, nt, preferred_element_type=jnp.float32)
                )
            halves = [f[:, i : i + HDIM] for f in found for i in range(0, BLOCK, HDIM)]
            peak = jnp.max(functools.reduce(jnp.maximum, halves), axis=1, keepdims=True)
            return found, peak

        def weigh(low, found, peak):
            left = beside(rows_of(block, 1, 3), rows_of(block, 1, 0))
            total = jnp.zeros((BLOCK, HDIM), jnp.float32)
            plain_weights = []
            moved_weights = []
            for step, scores in enumerate(found):
                right = beside(rows_of(low + step, 1, 1), rows_of(low + step, 1, 4))
                moved = lax.dot_general(left, right, nt, preferred_element_type=jnp.float32)
                weights = jnp.exp2((scores - peak) * exp2_scale)
                for i in range(0, BLOCK, HDIM):
                    total = total + weights[:, i : i + HDIM]
                plain_weights.append(weights.astype(jnp.bfloat16))
                moved_weights.append((weights * moved).astype(jnp.bfloat16))
            return total, beside(*plain_weights), beside(*moved_weights)

        def combine(low, width, plain_weights, moved_weights):
            value = rows_of(low, width, 2)
            sum_v = jnp.dot(
                plain_weights,
                beside(value, rows_of(low, width, 5)),
                preferred_element_type=jnp.float32,
            )
            sum_t = jnp.dot(
                moved_weights,
                beside(value, jnp.ones((width * BLOCK, HDIM), jnp.bfloat16)),
                preferred_element_type=jnp.float32,
            )
            return sum_v, sum_t

        def finish(total, sum_v, sum_t):
            inverse = 1.0 / jnp.sum(total, axis=1, keepdims=True)
            plain = sum_v[:, :HDIM] * inverse
            centre = sum_t[:, HDIM:] * inverse
            moved = scale * (sum_t[:, :HDIM] * inverse - centre * plain)
            moved = moved + sum_v[:, HDIM:] * inverse
            plain = plain.astype(jnp.bfloat16).astype(jnp.float32)
            moved = moved.astype(jnp.bfloat16).astype(jnp.float32)
            gate = jnp.where(second, gate_ref[1:2, :], gate_ref[0:1, :])
            rate = jnp.where(second, gate_ref[3:4, :], gate_ref[2:3, :])
            attended = (gate * plain).astype(jnp.bfloat16)
            attended_tangent = (rate * plain + gate * moved).astype(jnp.bfloat16)
            target = pl.ds(block * per, per)
            out_ref[target, 0] = attended.reshape(per, tokens, HDIM)
            out_ref[target, 1] = attended_tangent.reshape(per, tokens, HDIM)

        def with_width(width):
            first = jnp.minimum(low, blocks - width)
            found, peak = score(first, width)
            total, plain_weights, moved_weights = weigh(first, found, peak)
            finish(total, *combine(first, width, plain_weights, moved_weights))

        widths = [width for width in WIDTHS if width < blocks] + [blocks]
        for below, width in zip([0] + widths, widths):
            fits = (high - low > below) & (high - low <= width)
            pl.when(fits)(functools.partial(with_width, width))
        return carry

    lax.fori_loop(0, blocks, one_block, 0)


def attend(lengths, received, gates):
    groups, _, tokens, _ = received.shape
    length = groups * tokens
    in_vmem = pl.BlockSpec(memory_space=pltpu.VMEM)
    return pl.pallas_call(
        attention_kernel,
        in_specs=[pl.BlockSpec(memory_space=pltpu.SMEM)] + [in_vmem] * 2,
        out_specs=in_vmem,
        out_shape=jax.ShapeDtypeStruct((groups, 2, tokens, HDIM), jnp.bfloat16),
        scratch_shapes=[pltpu.VMEM((length, HDIM), jnp.bfloat16)] * 2,
        compiler_params=pltpu.CompilerParams(vmem_limit_bytes=32 * MIB),
        cost_estimate=pl.CostEstimate(
            flops=8 * length * length * HDIM,
            bytes_accessed=16 * length * HDIM,
            transcendentals=length * length,
        ),
    )(lengths, received, gates)


def exchange(array):
    return lax.all_to_all(array, "seq", split_axis=0, concat_axis=0, tiled=True)


def pick_rows(gate_table, rate_table, timesteps, groups):
    steps_here, width = gate_table.shape
    here = width // groups
    column = lax.axis_index("seq") * here
    tables = jnp.concatenate(
        [
            lax.dynamic_slice_in_dim(gate_table, column, here, 1),
            lax.dynamic_slice_in_dim(rate_table, column, here, 1),
        ],
        axis=1,
    )
    wanted = timesteps.reshape(-1) - lax.axis_index("fsdp") * steps_here
    one_hot = (wanted[:, None] == jnp.arange(steps_here, dtype=jnp.int32)[None, :]).astype(
        jnp.float32
    )
    picks = jnp.dot(one_hot, tables, precision=lax.Precision.HIGHEST)
    return picks.reshape(timesteps.shape[0], -1)


def behind_kernel(array, after, out):
    out[...] = array[...]


def behind(array, after):
    in_vmem = pl.BlockSpec(memory_space=pltpu.VMEM)
    return pl.pallas_call(
        behind_kernel,
        in_specs=[in_vmem, pl.BlockSpec(memory_space=pl.ANY)],
        out_specs=in_vmem,
        out_shape=jax.ShapeDtypeStruct(array.shape, array.dtype),
    )(array, after)


def halve(picks, bit, members):
    mine = (lax.axis_index("fsdp") // bit) % 2
    split = picks.reshape(2, bit, -1)
    kept = lax.dynamic_index_in_dim(split, mine, 0, keepdims=False)
    sent = lax.dynamic_index_in_dim(split, 1 - mine, 0, keepdims=False)
    return kept + lax.ppermute(sent, "fsdp", [(i, i ^ bit) for i in members])


def sum_picks(picks, core):
    size = lax.axis_size("fsdp")
    bit = size // 2
    while bit > 1:
        picks = halve(picks, bit, range(core, size, 2))
        bit //= 2
    return picks


def on_device(
    queries,
    key_states,
    value_states,
    query_tangent,
    key_tangent,
    value_tangent,
    gate_table,
    rate_table,
    timesteps,
    lengths,
):
    groups = lax.axis_size("seq")
    heads = queries.shape[2] // (groups * HDIM)
    arrays = (queries, key_states, value_states, query_tangent, key_tangent, value_tangent)
    picks = pick_rows(gate_table, rate_table, timesteps, groups)
    odd_sum = sum_picks(picks, 1)
    packed = pack(arrays, heads, odd_sum)
    even_sum = sum_picks(behind(picks, packed[-1]), 0)
    sums = jnp.where(lax.axis_index("fsdp") % 2 == 1, odd_sum, even_sum)
    mine = halve(sums, 1, range(lax.axis_size("fsdp")))
    mine = mine.reshape(2, 2, heads, HDIM)
    gates = mine.transpose(2, 1, 0, 3).reshape(heads, 4, HDIM)
    received = [exchange(part) for part in packed]
    parts = [attend(lengths, array, gate) for array, gate in zip(received, gates)]
    return tuple(unpack([exchange(part) for part in parts]))


def solution(mesh):
    rows = P("fsdp", "seq", None)
    table = P("fsdp", None)
    in_specs = (rows,) * 6 + (table, table, P(), table)
    return jax.shard_map(
        on_device, mesh=mesh, in_specs=in_specs, out_specs=(rows, rows), check_vma=False
    )
```

```python
import functools
import math

import jax
import jax.numpy as jnp
from jax import lax
from jax.experimental import pallas as pl
from jax.experimental.pallas import tpu as pltpu
from jax.sharding import PartitionSpec as P

HDIM = 128
BLOCK = 256
GROUPS_A_STEP = 8
ARRAYS = 6
MASKED = -1e30
WIDTHS = (2, 3, 4, 5, 6)
MIB = 1024 * 1024


def pack_kernel(heads, *refs):
    parts = refs[-heads:]
    for place, ref in enumerate(refs[:ARRAYS]):
        for group in range(GROUPS_A_STEP):
            for head in range(heads):
                column = (group * heads + head) * HDIM
                parts[head][group, place] = ref[0, :, column : column + HDIM]


def pack(arrays, heads, *after):
    _, tokens, width = arrays[0].shape
    groups = width // (heads * HDIM)
    part = (ARRAYS, tokens, HDIM)
    row_spec = pl.BlockSpec((1, tokens, GROUPS_A_STEP * heads * HDIM), lambda g: (0, 0, g))
    part_spec = pl.BlockSpec((GROUPS_A_STEP,) + part, lambda g: (g, 0, 0, 0))
    return pl.pallas_call(
        functools.partial(pack_kernel, heads),
        grid=(groups // GROUPS_A_STEP,),
        in_specs=[row_spec] * ARRAYS + [pl.BlockSpec(memory_space=pl.ANY)] * len(after),
        out_specs=[part_spec] * heads,
        out_shape=[jax.ShapeDtypeStruct((groups,) + part, jnp.bfloat16)] * heads,
        compiler_params=pltpu.CompilerParams(vmem_limit_bytes=56 * MIB),
        cost_estimate=pl.CostEstimate(
            flops=0, bytes_accessed=4 * ARRAYS * tokens * width, transcendentals=0
        ),
    )(*arrays, *after)


def unpack_kernel(*refs):
    heads = len(refs) - 2
    for head in range(heads):
        for group in range(GROUPS_A_STEP):
            column = (group * heads + head) * HDIM
            for place in range(2):
                refs[heads + place][0, :, column : column + HDIM] = refs[head][group, place]


def unpack(parts):
    groups, _, tokens, _ = parts[0].shape
    heads = len(parts)
    out = jax.ShapeDtypeStruct((1, tokens, groups * heads * HDIM), jnp.bfloat16)
    out_spec = pl.BlockSpec((1, tokens, GROUPS_A_STEP * heads * HDIM), lambda g: (0, 0, g))
    part_spec = pl.BlockSpec((GROUPS_A_STEP, 2, tokens, HDIM), lambda g: (g, 0, 0, 0))
    return pl.pallas_call(
        unpack_kernel,
        grid=(groups // GROUPS_A_STEP,),
        in_specs=[part_spec] * heads,
        out_specs=[out_spec, out_spec],
        out_shape=[out, out],
        compiler_params=pltpu.CompilerParams(vmem_limit_bytes=32 * MIB),
        cost_estimate=pl.CostEstimate(
            flops=0, bytes_accessed=8 * heads * groups * tokens * HDIM, transcendentals=0
        ),
    )(*parts)


def attention_kernel(len_ref, in_ref, gate_ref, out_ref, query_side, key_side):
    groups, _, tokens, _ = in_ref.shape
    length = groups * tokens
    first_len = len_ref[0, 0]
    scale = 1.0 / math.sqrt(HDIM)
    exp2_scale = scale * math.log2(math.e)
    nt = (((1,), (1,)), ((), ()))
    per = BLOCK // tokens
    blocks = length // BLOCK
    row = lax.broadcasted_iota(jnp.int32, (BLOCK, HDIM), 0)
    lane = lax.broadcasted_iota(jnp.int32, (BLOCK, HDIM), 1)

    def fill(block, carry):
        start = pl.multiple_of(block * BLOCK, BLOCK)
        own = jnp.where(start + row >= first_len, 1, 0)
        rows = pl.ds(start, BLOCK)
        query_side[rows, :] = jnp.where(lane == own, 1.0, 0.0).astype(jnp.bfloat16)
        key_side[rows, :] = jnp.where(lane == 1 - own, MASKED, 0.0).astype(jnp.bfloat16)
        return carry

    lax.fori_loop(0, blocks, fill, 0)

    def rows_of(block, count, place):
        found = in_ref[pl.ds(block * per, count * per), place]
        return found.reshape(count * BLOCK, HDIM)

    def beside(*pieces):
        return jnp.concatenate(pieces, axis=1)

    def one_block(block, carry):
        row0 = pl.multiple_of(block * BLOCK, BLOCK)
        second = row0 + row >= first_len
        low = jnp.where(row0 >= first_len, first_len // BLOCK, 0)
        high = jnp.where(row0 + BLOCK <= first_len, (first_len + BLOCK - 1) // BLOCK, blocks)

        def score(low, width):
            left = beside(rows_of(block, 1, 0), query_side[pl.ds(row0, BLOCK), :])
            found = []
            for step in range(width):
                start = pl.multiple_of((low + step) * BLOCK, BLOCK)
                right = beside(rows_of(low + step, 1, 1), key_side[pl.ds(start, BLOCK), :])
                found.append(
                    lax.dot_general(left, right, nt, preferred_element_type=jnp.float32)
                )
            halves = [f[:, i : i + HDIM] for f in found for i in range(0, BLOCK, HDIM)]
            peak = jnp.max(functools.reduce(jnp.maximum, halves), axis=1, keepdims=True)
            return found, peak

        def weigh(low, found, peak):
            left = beside(rows_of(block, 1, 3), rows_of(block, 1, 0))
            total = jnp.zeros((BLOCK, HDIM), jnp.float32)
            plain_weights = []
            moved_weights = []
            for step, scores in enumerate(found):
                right = beside(rows_of(low + step, 1, 1), rows_of(low + step, 1, 4))
                moved = lax.dot_general(left, right, nt, preferred_element_type=jnp.float32)
                weights = jnp.exp2((scores - peak) * exp2_scale)
                for i in range(0, BLOCK, HDIM):
                    total = total + weights[:, i : i + HDIM]
                plain_weights.append(weights.astype(jnp.bfloat16))
                moved_weights.append((weights * moved).astype(jnp.bfloat16))
            return total, beside(*plain_weights), beside(*moved_weights)

        def combine(low, width, plain_weights, moved_weights):
            value = rows_of(low, width, 2)
            sum_v = jnp.dot(
                plain_weights,
                beside(value, rows_of(low, width, 5)),
                preferred_element_type=jnp.float32,
            )
            sum_t = jnp.dot(
                moved_weights,
                beside(value, jnp.ones((width * BLOCK, HDIM), jnp.bfloat16)),
                preferred_element_type=jnp.float32,
            )
            return sum_v, sum_t

        def finish(total, sum_v, sum_t):
            inverse = 1.0 / jnp.sum(total, axis=1, keepdims=True)
            plain = sum_v[:, :HDIM] * inverse
            centre = sum_t[:, HDIM:] * inverse
            moved = scale * (sum_t[:, :HDIM] * inverse - centre * plain)
            moved = moved + sum_v[:, HDIM:] * inverse
            plain = plain.astype(jnp.bfloat16).astype(jnp.float32)
            moved = moved.astype(jnp.bfloat16).astype(jnp.float32)
            gate = jnp.where(second, gate_ref[1:2, :], gate_ref[0:1, :])
            rate = jnp.where(second, gate_ref[3:4, :], gate_ref[2:3, :])
            attended = (gate * plain).astype(jnp.bfloat16)
            attended_tangent = (rate * plain + gate * moved).astype(jnp.bfloat16)
            target = pl.ds(block * per, per)
            out_ref[target, 0] = attended.reshape(per, tokens, HDIM)
            out_ref[target, 1] = attended_tangent.reshape(per, tokens, HDIM)

        def with_width(width):
            first = jnp.minimum(low, blocks - width)
            found, peak = score(first, width)
            total, plain_weights, moved_weights = weigh(first, found, peak)
            finish(total, *combine(first, width, plain_weights, moved_weights))

        widths = [width for width in WIDTHS if width < blocks] + [blocks]
        for below, width in zip([0] + widths, widths):
            fits = (high - low > below) & (high - low <= width)
            pl.when(fits)(functools.partial(with_width, width))
        return carry

    lax.fori_loop(0, blocks, one_block, 0)


def attend(lengths, received, gates):
    groups, _, tokens, _ = received.shape
    length = groups * tokens
    in_vmem = pl.BlockSpec(memory_space=pltpu.VMEM)
    return pl.pallas_call(
        attention_kernel,
        in_specs=[pl.BlockSpec(memory_space=pltpu.SMEM)] + [in_vmem] * 2,
        out_specs=in_vmem,
        out_shape=jax.ShapeDtypeStruct((groups, 2, tokens, HDIM), jnp.bfloat16),
        scratch_shapes=[pltpu.VMEM((length, HDIM), jnp.bfloat16)] * 2,
        compiler_params=pltpu.CompilerParams(vmem_limit_bytes=32 * MIB),
        cost_estimate=pl.CostEstimate(
            flops=8 * length * length * HDIM,
            bytes_accessed=16 * length * HDIM,
            transcendentals=length * length,
        ),
    )(lengths, received, gates)


def exchange(array):
    return lax.all_to_all(array, "seq", split_axis=0, concat_axis=0, tiled=True)


def pick_rows(gate_table, rate_table, timesteps, groups):
    steps_here, width = gate_table.shape
    here = width // groups
    column = lax.axis_index("seq") * here
    tables = jnp.concatenate(
        [
            lax.dynamic_slice_in_dim(gate_table, column, here, 1),
            lax.dynamic_slice_in_dim(rate_table, column, here, 1),
        ],
        axis=1,
    )
    wanted = timesteps.reshape(-1) - lax.axis_index("fsdp") * steps_here
    one_hot = (wanted[:, None] == jnp.arange(steps_here, dtype=jnp.int32)[None, :]).astype(
        jnp.float32
    )
    picks = jnp.dot(one_hot, tables, precision=lax.Precision.HIGHEST)
    return picks.reshape(timesteps.shape[0], -1)


def behind_kernel(array, after, out):
    out[...] = array[...]


def behind(array, after):
    in_vmem = pl.BlockSpec(memory_space=pltpu.VMEM)
    return pl.pallas_call(
        behind_kernel,
        in_specs=[in_vmem, pl.BlockSpec(memory_space=pl.ANY)],
        out_specs=in_vmem,
        out_shape=jax.ShapeDtypeStruct(array.shape, array.dtype),
    )(array, after)


def halve(picks, bit, members):
    mine = (lax.axis_index("fsdp") // bit) % 2
    split = picks.reshape(2, bit, -1)
    kept = lax.dynamic_index_in_dim(split, mine, 0, keepdims=False)
    sent = lax.dynamic_index_in_dim(split, 1 - mine, 0, keepdims=False)
    return kept + lax.ppermute(sent, "fsdp", [(i, i ^ bit) for i in members])


def sum_picks(picks, core):
    size = lax.axis_size("fsdp")
    bit = size // 2
    while bit > 1:
        picks = halve(picks, bit, range(core, size, 2))
        bit //= 2
    return picks


def on_device(
    queries,
    key_states,
    value_states,
    query_tangent,
    key_tangent,
    value_tangent,
    gate_table,
    rate_table,
    timesteps,
    lengths,
):
    groups = lax.axis_size("seq")
    heads = queries.shape[2] // (groups * HDIM)
    arrays = (queries, key_states, value_states, query_tangent, key_tangent, value_tangent)
    picks = pick_rows(gate_table, rate_table, timesteps, groups)
    odd_sum = sum_picks(picks, 1)
    packed = pack(arrays, heads, odd_sum)
    even_sum = sum_picks(behind(picks, packed[-1]), 0)
    sums = jnp.where(lax.axis_index("fsdp") % 2 == 1, odd_sum, even_sum)
    mine = halve(sums, 1, range(lax.axis_size("fsdp")))
    mine = mine.reshape(2, 2, heads, HDIM)
    gates = mine.transpose(2, 1, 0, 3).reshape(heads, 4, HDIM)
    received = [exchange(part) for part in packed]
    parts = [attend(lengths, array, gate) for array, gate in zip(received, gates)]
    return tuple(unpack([exchange(part) for part in parts]))


def solution(mesh):
    rows = P("fsdp", "seq", None)
    table = P("fsdp", None)
    in_specs = (rows,) * 6 + (table, table, P(), table)
    return jax.shard_map(
        on_device, mesh=mesh, in_specs=in_specs, out_specs=(rows, rows), check_vma=False
    )
```
